256 devices in a mesh: pipe: 16 (over y, z_hi, core), expert: 4 (over x), shard: 4 (over z_lo).
Axes of the slice: x: 4, y: 4, z: 8 (z_hi: 2, z_lo: 4; z = z_hi * 4 + z_lo), core: 2. Of those that a mesh axis runs over, the one named last changes fastest.
Arguments:
- tokens: bfloat16 [16, 2048, 1792], P('pipe', ('expert', 'shard')), may hold values from -6 to 6
- grad_out: bfloat16 [16, 2048, 1792], P('pipe', ('expert', 'shard')), may hold values from -6 to 6
- expert_ids: int32 [16, 2048, 2], P('pipe', ('expert', 'shard')), may hold values from 0 to 3, all different within a row; in each aligned block of 128 rows (0 to 127, 128 to 255, ..., all dimensions but the last counted through in order) at most 96 rows name the same one
- gates: float32 [16, 2048, 2], P('pipe', ('expert', 'shard')), may hold values from 0.1 to 1
- weights: bfloat16 [16, 4, 1280, 3, 1792], P('pipe', 'expert', 'shard'), may hold values from -0.125 to 0.125
Outputs:
- grad_prev: bfloat16 [16, 2048, 1792], P('pipe', ('expert', 'shard'))
- grad_weights: bfloat16 [16, 4, 1280, 3, 1792], P('pipe', 'expert', 'shard')
The draws below stay inside these ranges and needn't reach their ends.
Inputs may be any that keep to these rules, and one draw needn't show every extreme that they name: `expert_ids`: each token names 2 different experts. The 128 tokens of one device name one expert at most 96 times, and in every draw some device's tokens name some expert exactly 96 times.
All inputs are finite; a program needn't handle non-finite values.
Results may differ from the reference program's by a relative error of at most 0.014.
Values may be sent and summed in bfloat16 or wider, within the bound.
No kernel may reach another device: no remote copies, remote signals or barrier semaphores. Data moves between devices by JAX's collectives and lax.ppermute only.
A program may use at most 128 MiB of HBM per device.

```python
import math
import jax
import jax.numpy as jnp
import numpy as np
from jax import lax

D = 1792
F = 1280
TOPK = 2
TOK_DEV = 128
EXPERTS = 4
CAP = 96
TOK_SECTION = 2048
SECTIONS = 16
N_EXPERT = 4
N_SHARD = 4


def level_of(own_key, dims, cuts, low, top_value):
    gain = 1.0
    for axis_at, blocks in cuts:
        steps = jax.random.uniform(jax.random.fold_in(jax.random.fold_in(own_key, 6), axis_at), (blocks,), jnp.float32, low / len(cuts), top_value / len(cuts))
        gain = gain * jnp.repeat(jnp.exp(steps), dims[axis_at] // blocks).reshape((-1,) + (1,) * (len(dims) - 1 - axis_at))
    return gain


def shared_out(rng, own, number, rows, count, top, reach, slope):
    ranking = jax.random.permutation(rng, count)
    heavy_load, ordinary = load_shares(count, rows * top, reach, slope, True), load_shares(count, rows * top, reach, slope, False)
    places = jnp.arange(count)

    def named(sizes, offset_by):
        used = int((sizes > 0).sum())
        fixed = max(1, used // 4)
        shifted = fixed + (places - fixed + offset_by * (used - fixed)) % max(1, count - fixed)
        return jnp.zeros((count,), jnp.int32).at[ranking[jnp.where(places < fixed, places, shifted)]].set(jnp.asarray(sizes, jnp.int32))

    sizes = jnp.where(number % 4 == 0, named(heavy_load, number // 4), named(ordinary, number - number // 4 - 1))
    mixed = jax.random.permutation(jax.random.fold_in(own, 3), count)
    source_of, taker = mixed[0:count // 2 * 2:2], mixed[1:count // 2 * 2:2]
    room = jnp.minimum(sizes[source_of] - 1, reach - sizes[taker]) // 2
    room = jnp.where((source_of == ranking[0]) | (taker == ranking[0]) | (sizes[taker] == 0), 0, jnp.maximum(room, 0))
    shifted = jax.random.randint(jax.random.fold_in(own, 4), (count // 2,), 0, 1 << 20) % (room + 1)
    sizes = sizes.at[source_of].add(-shifted).at[taker].add(shifted)
    members = jnp.searchsorted(jnp.cumsum(sizes), jnp.arange(rows * top), side="right").astype(jnp.int32)
    listing = members.reshape(top, rows).T
    listing = listing[jax.random.permutation(jax.random.fold_in(own, 1), rows)]
    offset_by = jax.random.randint(jax.random.fold_in(own, 2), (rows, 1), 0, top)
    return jnp.take_along_axis(listing, (jnp.arange(top)[None, :] + offset_by) % top, axis=1)


def load_shares(number_of, total, reach, slope, full):
    portions = [(1 << 20) // math.isqrt(standing ** slope) + 1 for standing in range(1, number_of + 1)]
    largest = reach if full else min(reach, max(-(-total // number_of), total * portions[0] // sum(portions)))
    least = 1 if total - largest >= number_of - 1 else 0
    holding, surplus = [largest] + [least] * (number_of - 1), total - largest - least * (number_of - 1)
    while surplus > 0:
        movable = [i for i in range(1, number_of) if holding[i] < largest] or [i for i in range(1, number_of) if holding[i] < reach]
        pool, left = sum([portions[i] for i in movable]), surplus
        for i in movable:
            addition = min(reach - holding[i], max(1, left * portions[i] // pool), surplus)
            holding[i] = holding[i] + addition
            surplus = surplus - addition
    return np.array(holding)


def bell_draw(key, dims, scale, most, shards=(), held_as=jnp.bfloat16):
    loudness = level_of(key, dims, shards, -0.22, 0.18) if shards else 1.0
    drawn = jax.random.normal(key, dims, jnp.float32) * scale * loudness
    return jnp.minimum(jnp.maximum(drawn, -most), most).astype(held_as)


def setup_inputs(seed: int = 0) -> dict:
    streams_of = jax.random.split(jax.random.key(seed), 6)
    tokens = bell_draw(streams_of[0], (SECTIONS, TOK_SECTION, D), 1.0, 6.0, ((0, 16), (1, 16)))
    grad_out = bell_draw(streams_of[1], (SECTIONS, TOK_SECTION, D), 1.0, 6.0, ((0, 16), (1, 16)))
    expert_ids_keys = jax.random.split(jax.random.fold_in(streams_of[2], 1), SECTIONS * TOK_SECTION // TOK_DEV)
    expert_ids_turns = jax.random.permutation(jax.random.fold_in(streams_of[2], 3), SECTIONS * TOK_SECTION // TOK_DEV)
    expert_ids = jax.vmap(lambda own, number: shared_out(jax.random.fold_in(streams_of[2], 2), own, number, TOK_DEV, EXPERTS, TOPK, CAP, 1))(expert_ids_keys, expert_ids_turns).reshape((SECTIONS, TOK_SECTION, TOPK))
    gates = jnp.clip(0.1 + 0.9 * jax.random.uniform(streams_of[3], (SECTIONS, TOK_SECTION, TOPK), jnp.float32) ** level_of(streams_of[3], (SECTIONS, TOK_SECTION, TOPK), ((0, 16), (1, 16)), -0.2, 0.2), 0.1, 1.0)
    weights = bell_draw(streams_of[4], (SECTIONS, EXPERTS, F, 3, D), D ** -0.5, 0.125, ((0, 16), (1, 4), (2, 4)))
    return dict(tokens=tokens, grad_out=grad_out, expert_ids=expert_ids, gates=gates, weights=weights)


def placing_for(routes):
    flat_routes = routes.reshape(-1)
    onehot = (flat_routes[:, None] == jnp.arange(N_EXPERT, dtype=jnp.int32)[None, :]).astype(jnp.int32)
    before = jnp.cumsum(onehot, axis=0) - onehot
    position = jnp.sum(before * onehot, axis=1).astype(jnp.int32)
    target = flat_routes * CAP + position
    return (target[None, :] == jnp.arange(N_EXPERT * CAP, dtype=jnp.int32)[:, None]).astype(jnp.float32)


def reference(tokens, grad_out, expert_ids, gates, weights):
    device_count = N_EXPERT * N_SHARD
    slots_all = N_EXPERT * CAP

    def one_section(section_args):
        section_tokens, section_grad, section_routes, section_gates, section_weights = section_args
        blocks_in = section_tokens.reshape(device_count, TOK_DEV, D)
        placing = jax.vmap(placing_for)(section_routes.reshape(device_count, TOK_DEV, TOPK))
        placing_tok = placing.reshape(device_count, slots_all, TOK_DEV, TOPK).sum(axis=3)
        send_in = jnp.einsum("nst,ntd->nsd", placing_tok, blocks_in.astype(jnp.float32)).astype(jnp.bfloat16)
        cotangent = (section_gates[:, :, None] * section_grad[:, None, :].astype(jnp.float32)).astype(jnp.bfloat16)
        cotangent = cotangent.reshape(device_count, TOK_DEV * TOPK, D)
        send_cot = jnp.einsum("nsr,nrd->nsd", placing, cotangent.astype(jnp.float32)).astype(jnp.bfloat16)
        send_in = send_in.reshape(N_EXPERT, N_SHARD, N_EXPERT, CAP, D)
        send_cot = send_cot.reshape(N_EXPERT, N_SHARD, N_EXPERT, CAP, D)

        def expert_work(expert_index):
            rows_in = jnp.take(send_in, expert_index, axis=2).transpose(1, 0, 2, 3).reshape(-1, D)
            rows_cot = jnp.take(send_cot, expert_index, axis=2).transpose(1, 0, 2, 3).reshape(-1, D)
            expert_weights = jnp.take(section_weights, expert_index, axis=0)
            w_gate = expert_weights[:, 0, :]
            w_up = expert_weights[:, 1, :]
            w_down = expert_weights[:, 2, :]
            pre_gate = jnp.dot(rows_in, w_gate.T, preferred_element_type=jnp.float32)
            pre_up = jnp.dot(rows_in, w_up.T, preferred_element_type=jnp.float32)
            sigmoid_gate = jax.nn.sigmoid(pre_gate)
            gated = pre_gate * sigmoid_gate
            hidden = (gated * pre_up).astype(jnp.bfloat16)
            grad_hidden = jnp.dot(rows_cot, w_down.T, preferred_element_type=jnp.float32)
            grad_gate = (grad_hidden * pre_up * sigmoid_gate * (1.0 + pre_gate * (1.0 - sigmoid_gate))).astype(jnp.bfloat16)
            grad_up = (grad_hidden * gated).astype(jnp.bfloat16)
            route_grad = (jnp.dot(grad_gate, w_gate, preferred_element_type=jnp.float32)
                          + jnp.dot(grad_up, w_up, preferred_element_type=jnp.float32)).astype(jnp.bfloat16)
            split_in = rows_in.reshape(N_SHARD, -1, D).astype(jnp.float32)
            split_cot = rows_cot.reshape(N_SHARD, -1, D).astype(jnp.float32)
            part_gate = jnp.einsum("grf,grd->gfd", grad_gate.reshape(N_SHARD, -1, F).astype(jnp.float32), split_in)
            part_up = jnp.einsum("grf,grd->gfd", grad_up.reshape(N_SHARD, -1, F).astype(jnp.float32), split_in)
            part_down = jnp.einsum("grf,grd->gfd", hidden.reshape(N_SHARD, -1, F).astype(jnp.float32), split_cot)
            partial_value = jnp.stack([part_gate, part_up, part_down], axis=2).astype(jnp.bfloat16)
            partial_value = lax.optimization_barrier(partial_value).astype(jnp.float32)
            grad_expert = jnp.sum(partial_value, axis=0).astype(jnp.bfloat16)
            route_grad = route_grad.reshape(N_SHARD, N_EXPERT, CAP, D).transpose(1, 0, 2, 3).reshape(device_count, CAP, D)
            return route_grad, grad_expert

        route_grads, grad_section = lax.map(expert_work, jnp.arange(N_EXPERT, dtype=jnp.int32))
        returned = route_grads.transpose(1, 0, 2, 3).reshape(device_count, slots_all, D)
        per_route = jnp.einsum("nsr,nsd->nrd", placing, returned.astype(jnp.float32))
        input_grad = per_route.reshape(device_count, TOK_DEV, TOPK, D).sum(axis=2).astype(jnp.bfloat16)
        return input_grad.reshape(device_count * TOK_DEV, D), grad_section

    input_grads, grad_weights = lax.map(one_section, (tokens, grad_out, expert_ids, gates, weights))
    grad_prev = jnp.roll(input_grads, -1, axis=0)
    return grad_prev, grad_weights
```

```python
import jax
import jax.numpy as jnp
from jax import lax
from jax.sharding import PartitionSpec as P

X_AXIS = "expert"
Z_AXIS = "shard"


def send(block, axis, distance):
    n = lax.axis_size(axis)
    return lax.ppermute(block, axis, [(i, (i + distance) % n) for i in range(n)])


def after(value, *earlier):
    return lax.optimization_barrier((value, *earlier))[0]


def gates_by_source(expert_ids, gates):
    n_x, n_z = lax.axis_size(X_AXIS), lax.axis_size(Z_AXIS)
    experts = jnp.arange(n_x, dtype=jnp.int32)
    dense = jnp.sum(
        jnp.where(expert_ids[None] == experts[:, None, None], gates[None], 0.0), axis=2
    )
    tokens_here = dense.shape[1]
    outgoing = jnp.broadcast_to(dense[:, None], (n_x, n_z, tokens_here))
    incoming = lax.all_to_all(
        outgoing.reshape(n_x * n_z, 1, tokens_here),
        (X_AXIS, Z_AXIS),
        split_axis=0,
        concat_axis=0,
        tiled=True,
    ).reshape(n_x, n_z, tokens_here)
    return incoming


def shards(tokens, grad_out, expert_ids, gates, weights):
    tokens, grad_out = tokens[0], grad_out[0]
    rows, width = tokens.shape
    half = width // 2
    mine_x, mine_z = lax.axis_index(X_AXIS), lax.axis_index(Z_AXIS)
    gate_table = gates_by_source(expert_ids[0], gates[0])
    pieces = jnp.transpose(weights[0, 0], (1, 0, 2))
    units = pieces.shape[1]
    w_in = pieces[:2].reshape(2 * units, width)
    w_down = pieces[2]

    own = jnp.concatenate([tokens, grad_out], axis=0)
    z_prev = send(own, Z_AXIS, 1)
    z_next = send(after(own, z_prev), Z_AXIS, -1)
    z_far = send(after(own, z_next), Z_AXIS, 2)

    def slab_in(block):
        prev = send(block, X_AXIS, 1)
        succ = send(block, X_AXIS, -1)
        far_tok = send(prev[:rows], X_AXIS, 1)
        far_cot = send(succ[rows:], X_AXIS, -1)
        tok = jnp.concatenate([block[:rows], prev[:rows], succ[:rows], far_tok], axis=0)
        cot = jnp.concatenate([block[rows:], prev[rows:], succ[rows:], far_cot], axis=0)
        return tok, cot

    def slab_gates(z_distance):
        column = jnp.take(gate_table, (mine_z - z_distance) % 4, axis=1)
        order = [0, 1, -1, 2]
        return jnp.concatenate(
            [jnp.take(column, (mine_x - d) % 4, axis=0) for d in order], axis=0
        )[:, None]

    def slab_work(tok, cot, gate):
        pre = jnp.einsum("rd,fd->rf", tok, w_in, preferred_element_type=jnp.float32)
        grad_hidden = gate * jnp.einsum("rd,fd->rf", cot, w_down, preferred_element_type=jnp.float32)
        pre_gate, pre_up = pre[:, :units], pre[:, units:]
        sig = jax.nn.sigmoid(pre_gate)
        gated = pre_gate * sig
        hidden = (gate * gated * pre_up).astype(jnp.bfloat16)
        grad_gate = (grad_hidden * pre_up * sig * (1.0 + pre_gate * (1.0 - sig))).astype(jnp.bfloat16)
        grad_up = (grad_hidden * gated).astype(jnp.bfloat16)
        grads = jnp.concatenate([grad_gate, grad_up], axis=1)
        back = jnp.dot(grads, w_in, preferred_element_type=jnp.float32).astype(jnp.bfloat16)
        return grads, hidden, back

    def add(a, b):
        return (a.astype(jnp.float32) + b.astype(jnp.float32)).astype(jnp.bfloat16)

    def slab_out(back):
        mine, prev, succ, far = [back[i * rows : (i + 1) * rows] for i in range(4)]
        from_prev = send(far[:, :half], X_AXIS, 1)
        from_succ = send(far[:, half:], X_AXIS, -1)
        to_succ = jnp.concatenate([add(succ[:, :half], from_prev), succ[:, half:]], axis=1)
        to_prev = jnp.concatenate([prev[:, :half], add(prev[:, half:], from_succ)], axis=1)
        got_prev = send(to_succ, X_AXIS, 1)
        got_succ = send(to_prev, X_AXIS, -1)
        return mine.astype(jnp.float32) + got_prev.astype(jnp.float32) + got_succ.astype(jnp.float32)

    toks, cots, grads, hiddens, totals = [], [], [], [], []
    for distance, block in ((0, own), (1, z_prev), (-1, z_next), (2, z_far)):
        tok, cot = slab_in(block)
        grad, hidden, back = slab_work(tok, cot, slab_gates(distance))
        total = slab_out(back)
        if distance:
            total = send(total.astype(jnp.bfloat16), Z_AXIS, -distance)
        toks.append(tok)
        cots.append(cot)
        grads.append(grad)
        hiddens.append(hidden)
        totals.append(total.astype(jnp.float32))

    input_grad = sum(totals).astype(jnp.bfloat16)
    grad_prev = send(input_grad[None], "pipe", -1)

    all_tok, all_cot = jnp.concatenate(toks, axis=0), jnp.concatenate(cots, axis=0)
    all_grad, all_hidden = jnp.concatenate(grads, axis=0), jnp.concatenate(hiddens, axis=0)
    grad_in = jnp.einsum("rf,rd->fd", all_grad, all_tok, preferred_element_type=jnp.float32)
    grad_down = jnp.einsum("rf,rd->fd", all_hidden, all_cot, preferred_element_type=jnp.float32)
    grad_weights = jnp.concatenate(
        [grad_in.astype(jnp.bfloat16), grad_down.astype(jnp.bfloat16)], axis=0
    ).reshape(3, units, width)
    return grad_prev, jnp.transpose(grad_weights, (1, 0, 2))[None, None]


def solution(mesh):
    return jax.shard_map(
        shards,
        mesh=mesh,
        in_specs=(
            P("pipe", ("expert", "shard"), None),
            P("pipe", ("expert", "shard"), None),
            P("pipe", ("expert", "shard"), None),
            P("pipe", ("expert", "shard"), None),
            P("pipe", "expert", "shard", None, None),
        ),
        out_specs=(P("pipe", ("expert", "shard"), None), P("pipe", "expert", "shard", None, None)),
        check_vma=False,
    )
```

```python
import jax
import jax.numpy as jnp
from jax import lax
from jax.sharding import PartitionSpec as P

X_AXIS = "expert"
Z_AXIS = "shard"


def send(block, axis, distance):
    n = lax.axis_size(axis)
    return lax.ppermute(block, axis, [(i, (i + distance) % n) for i in range(n)])


def after(value, *earlier):
    return lax.optimization_barrier((value, *earlier))[0]


def gates_by_source(expert_ids, gates):
    n_x, n_z = lax.axis_size(X_AXIS), lax.axis_size(Z_AXIS)
    experts = jnp.arange(n_x, dtype=jnp.int32)
    dense = jnp.sum(
        jnp.where(expert_ids[None] == experts[:, None, None], gates[None], 0.0), axis=2
    )
    tokens_here = dense.shape[1]
    outgoing = jnp.broadcast_to(dense[:, None], (n_x, n_z, tokens_here))
    incoming = lax.all_to_all(
        outgoing.reshape(n_x * n_z, 1, tokens_here),
        (X_AXIS, Z_AXIS),
        split_axis=0,
        concat_axis=0,
        tiled=True,
    ).reshape(n_x, n_z, tokens_here)
    return incoming


def shards(tokens, grad_out, expert_ids, gates, weights):
    tokens, grad_out = tokens[0], grad_out[0]
    rows, width = tokens.shape
    half = width // 2
    mine_x, mine_z = lax.axis_index(X_AXIS), lax.axis_index(Z_AXIS)
    pieces = jnp.transpose(weights[0, 0], (1, 0, 2))
    units = pieces.shape[1]
    w_in = pieces[:2].reshape(2 * units, width)
    w_down = pieces[2]
    own = jnp.concatenate([tokens, grad_out], axis=0)

    def hop_one(block):
        return send(block, X_AXIS, 1), send(block, X_AXIS, -1)

    def hop_two(prev, succ):
        return send(prev[:rows], X_AXIS, 1), send(succ[rows:], X_AXIS, -1)

    def near_rows(block, prev, succ):
        return tuple(
            jnp.concatenate([part[cut] for part in (block, prev, succ)], axis=0)
            for cut in (slice(0, rows), slice(rows, None))
        )

    def gates_of(table, z_distance, x_distances):
        column = jnp.take(table, (mine_z - z_distance) % 4, axis=1)
        return jnp.concatenate(
            [jnp.take(column, (mine_x - d) % 4, axis=0) for d in x_distances], axis=0
        )[:, None]

    def work(tok, cot, gate):
        pre = jnp.einsum("rd,fd->rf", tok, w_in, preferred_element_type=jnp.float32)
        grad_hidden = gate * jnp.einsum("rd,fd->rf", cot, w_down, preferred_element_type=jnp.float32)
        pre_gate, pre_up = pre[:, :units], pre[:, units:]
        sig = jax.nn.sigmoid(pre_gate)
        gated = pre_gate * sig
        hidden = (gate * gated * pre_up).astype(jnp.bfloat16)
        grad_gate = (grad_hidden * pre_up * sig * (1.0 + pre_gate * (1.0 - sig))).astype(jnp.bfloat16)
        grad_up = (grad_hidden * gated).astype(jnp.bfloat16)
        grads = jnp.concatenate([grad_gate, grad_up], axis=1)
        back = jnp.dot(grads, w_in, preferred_element_type=jnp.float32).astype(jnp.bfloat16)
        return grads, hidden, back

    def near_work(table, z_distance, *blocks):
        tok, cot = near_rows(*blocks)
        return (tok, cot) + work(tok, cot, gates_of(table, z_distance, (0, 1, -1)))

    def far_work(table, z_distance, tok, cot):
        return (tok, cot) + work(tok, cot, gates_of(table, z_distance, (2,)))

    def add(*parts):
        return sum(p.astype(jnp.float32) for p in parts).astype(jnp.bfloat16)

    def out_one(far):
        return send(far[:, :half], X_AXIS, 1), send(far[:, half:], X_AXIS, -1)

    def out_two(near, from_prev, from_succ):
        prev, succ = near[rows : 2 * rows], near[2 * rows :]
        to_succ = jnp.concatenate([add(succ[:, :half], from_prev), succ[:, half:]], axis=1)
        to_prev = jnp.concatenate([prev[:, :half], add(prev[:, half:], from_succ)], axis=1)
        return send(to_succ, X_AXIS, 1), send(to_prev, X_AXIS, -1)

    n_pipe, n_z = lax.axis_size("pipe"), lax.axis_size(Z_AXIS)

    def home(total, z_distance):
        route = [
            (p * n_z + z, (p - 1) % n_pipe * n_z + (z - z_distance) % n_z)
            for p in range(n_pipe)
            for z in range(n_z)
        ]
        return lax.ppermute(total, ("pipe", Z_AXIS), route)

    z_prev = send(own, Z_AXIS, 1)
    first0 = hop_one(own)
    second0 = hop_two(*first0)
    table = gates_by_source(after(expert_ids[0], *first0), gates[0])
    near0 = near_work(table, 0, own, *first0)

    first1 = hop_one(after(z_prev, *first0))
    z_next = send(after(own, z_prev), Z_AXIS, -1)
    far0 = far_work(table, 0, *second0)

    second1 = hop_two(*first1)
    first2 = hop_one(after(z_next, *first1))
    z_far_tok = send(after(z_prev[:rows], z_next), Z_AXIS, 1)
    z_far_cot = send(z_next[rows:], Z_AXIS, -1)
    near1 = near_work(table, 1, z_prev, *first1)
    far1 = far_work(table, 1, *second1)
    home1_near = send(near1[4], Z_AXIS, -1)
    home1_far = send(far1[4], Z_AXIS, -1)

    second2 = hop_two(*first2)
    z_far = jnp.concatenate([z_far_tok, z_far_cot], axis=0)
    first3 = hop_one(after(z_far, *first2))
    near2 = near_work(table, -1, z_next, *first2)
    far2 = far_work(table, -1, *second2)
    one2 = out_one(far2[4])

    second3 = hop_two(*first3)
    near3 = near_work(table, 2, z_far, *first3)
    two2 = out_two(near2[4], *one2)
    far3 = far_work(table, 2, *second3)
    one3 = out_one(far3[4])
    near_own = add(near0[4], home1_near)
    far_own = add(far0[4], home1_far)
    one0 = out_one(far_own)
    total2 = home(add(near2[4][:rows], *two2), -1)
    two3 = out_two(near3[4], *one3)
    two0 = out_two(near_own, *one0)
    total3 = home(add(near3[4][:rows], *two3), 2)
    total0 = home(add(near_own[:rows], *two0), 0)
    grad_prev = add(total0, total2, total3)[None]

    fars = [jnp.concatenate(list(parts), axis=0) for parts in zip(far0, far1, far2, far3)]
    parts = [0.0, 0.0, 0.0]
    for tok, cot, grads, hidden, _ in (near0, near1, near2, near3, fars):
        pairs = ((grads[:, :units], tok), (grads[:, units:], tok), (hidden, cot))
        parts = [
            part + jnp.einsum("rf,rd->fd", left, right, preferred_element_type=jnp.float32)
            for part, (left, right) in zip(parts, pairs)
        ]
    grad_weights = jnp.transpose(jnp.stack([p.astype(jnp.bfloat16) for p in parts]), (1, 0, 2))
    return grad_prev, grad_weights[None, None]


def solution(mesh):
    return jax.shard_map(
        shards,
        mesh=mesh,
        in_specs=(
            P("pipe", ("expert", "shard"), None),
            P("pipe", ("expert", "shard"), None),
            P("pipe", ("expert", "shard"), None),
            P("pipe", ("expert", "shard"), None),
            P("pipe", "expert", "shard", None, None),
        ),
        out_specs=(P("pipe", ("expert", "shard"), None), P("pipe", "expert", "shard", None, None)),
        check_vma=False,
    )
```

```python
import functools

import jax
import jax.numpy as jnp
from jax import lax
from jax.experimental import pallas as pl
from jax.experimental.pallas import tpu as pltpu
from jax.sharding import PartitionSpec as P

X_AXIS = "expert"
Z_AXIS = "shard"


def send(block, axis, distance):
    n = lax.axis_size(axis)
    return lax.ppermute(block, axis, [(i, (i + distance) % n) for i in range(n)])


def after(value, *earlier):
    return lax.optimization_barrier((value, *earlier))[0]


CONTRACT_LAST = (((1,), (1,)), ((), ()))
MIB = 1 << 20


def _slab_kernel(places, gate_rows, groups, n_blocks, add_up, more, *refs):
    blocks, (gate, w), refs = refs[:n_blocks], refs[n_blocks : n_blocks + 2], refs[n_blocks + 2 :]
    n = len(places)
    n_back = sum(2 if cut else 1 for _, cut in groups)
    if more:
        earlier, refs = refs[0], refs[1:]
    if add_up:
        grad_w, refs = refs[0], refs[1:]
    else:
        grads, hidden, refs = refs[0], refs[1], refs[2:]
    backs, refs = refs[:n_back], refs[n_back:]
    tok_v, cot_v, w_v, gate_v, g_v, h_v, back_v, sem_in, sem_out = refs[:9]
    rows = tok_v.shape[0] // n
    units = w.shape[0] // 3
    width = w.shape[1]

    toks, cots, gate_copies = [], [], []
    for p, (tb, tr, cb, cr) in enumerate(places):
        here = pl.ds(p * rows, rows)
        toks.append(pltpu.make_async_copy(blocks[tb].at[pl.ds(tr, rows)], tok_v.at[here], sem_in.at[p]))
        cots.append(
            pltpu.make_async_copy(blocks[cb].at[pl.ds(cr, rows)], cot_v.at[here], sem_in.at[n + p])
        )
        gate_copies.append(
            pltpu.make_async_copy(
                gate.at[pl.ds(gate_rows[p], rows)], gate_v.at[here], sem_in.at[2 * n + p]
            )
        )
    w_in = pltpu.make_async_copy(
        w.at[pl.ds(0, 2 * units)], w_v.at[pl.ds(0, 2 * units)], sem_in.at[3 * n]
    )
    w_down = pltpu.make_async_copy(
        w.at[pl.ds(2 * units, units)], w_v.at[pl.ds(2 * units, units)], sem_in.at[3 * n + 1]
    )
    for copy in (*toks, w_in, *cots, w_down, *gate_copies):
        copy.start()
    if more:
        before = pltpu.make_async_copy(earlier, refs[9], sem_in.at[3 * n + 2])
        before.start()
    for copy in (*toks, w_in):
        copy.wait()
    w_gate, w_up = w_v[pl.ds(0, units)], w_v[pl.ds(units, units)]
    tok = tok_v[...]
    pre_gate = lax.dot_general(tok, w_gate, CONTRACT_LAST, preferred_element_type=jnp.float32)
    pre_up = lax.dot_general(tok, w_up, CONTRACT_LAST, preferred_element_type=jnp.float32)
    sig = jax.nn.sigmoid(pre_gate)
    gated = pre_gate * sig
    slope = sig * (1.0 + pre_gate * (1.0 - sig))
    for copy in (*cots, w_down, *gate_copies):
        copy.wait()
    gate_here = gate_v[...]
    grad_hidden = gate_here * lax.dot_general(
        cot_v[...], w_v[pl.ds(2 * units, units)], CONTRACT_LAST, preferred_element_type=jnp.float32
    )
    hid = (gate_here * gated * pre_up).astype(jnp.bfloat16)
    grad_gate = (grad_hidden * pre_up * slope).astype(jnp.bfloat16)
    grad_up = (grad_hidden * gated).astype(jnp.bfloat16)
    outs = []
    if add_up:
        g_v[pl.ds(0, units)] = grad_gate.T
        g_v[pl.ds(units, units)] = grad_up.T
        h_v[...] = hid.T
    else:
        h_v[...] = hid
        g_v[0] = grad_gate
        g_v[1] = grad_up
        outs = [
            pltpu.make_async_copy(g_v, grads, sem_out.at[0]),
            pltpu.make_async_copy(h_v, hidden, sem_out.at[1]),
        ]
    for copy in outs:
        copy.start()
    half = width // 2
    for c in range(2):
        cols = pl.ds(c * half, half)
        back = jnp.dot(grad_gate, w_v[pl.ds(0, units), cols], preferred_element_type=jnp.float32)
        back += jnp.dot(grad_up, w_v[pl.ds(units, units), cols], preferred_element_type=jnp.float32)
        back_v[:, cols] = back.astype(jnp.bfloat16)
        at, row = 0, 0
        for k, (count, cut) in enumerate(groups):
            here = back_v.at[pl.ds(row, count * rows), cols]
            there = backs[at + c] if cut else backs[at].at[:, cols]
            outs.append(pltpu.make_async_copy(here, there, sem_out.at[2 + 2 * k + c]))
            outs[-1].start()
            at, row = at + (2 if cut else 1), row + count * rows
    if add_up:
        out_v = refs[9]
        if more:
            before.wait()

        def tile(i, _):
            cols = pl.ds(pl.multiple_of(i * 256, 256), 256)
            left = jnp.dot(g_v[...], tok_v[:, cols], preferred_element_type=jnp.float32)
            right = jnp.dot(h_v[...], cot_v[:, cols], preferred_element_type=jnp.float32)
            if more:
                left += out_v[pl.ds(0, 2 * units), cols].astype(jnp.float32)
                right += out_v[pl.ds(2 * units, units), cols].astype(jnp.float32)
            out_v[pl.ds(0, 2 * units), cols] = left.astype(jnp.bfloat16)
            out_v[pl.ds(2 * units, units), cols] = right.astype(jnp.bfloat16)
            return 0

        lax.fori_loop(0, width // 256, tile, 0)
        outs.append(pltpu.make_async_copy(out_v, grad_w, sem_out.at[0]))
        outs[-1].start()
    for copy in outs:
        copy.wait()


def slab_work(pieces, gate, gate_rows, w, groups, add_up=False, earlier=None):
    rows, width = 128, w.shape[1]
    units = w.shape[0] // 3
    blocks, places = [], []

    def place(array):
        for i, known in enumerate(blocks):
            if known is array:
                return i
        blocks.append(array)
        return len(blocks) - 1

    for tok, tr, cot, cr in pieces:
        places.append((place(tok), tr, place(cot), cr))
    n = len(pieces)
    total = n * rows
    if add_up:
        out_shape = [jax.ShapeDtypeStruct((3 * units, width), jnp.bfloat16)]
        keep = [pltpu.VMEM((2 * units, total), jnp.bfloat16), pltpu.VMEM((units, total), jnp.bfloat16)]
    else:
        out_shape = [
            jax.ShapeDtypeStruct((2, total, units), jnp.bfloat16),
            jax.ShapeDtypeStruct((total, units), jnp.bfloat16),
        ]
        keep = [pltpu.VMEM((2, total, units), jnp.bfloat16), pltpu.VMEM((total, units), jnp.bfloat16)]
    n_first = len(out_shape)
    for count, cut in groups:
        shape = (count * rows, width // 2) if cut else (count * rows, width)
        out_shape += [jax.ShapeDtypeStruct(shape, jnp.bfloat16)] * (2 if cut else 1)
    extra = [] if earlier is None else [earlier]
    hbm = pl.BlockSpec(memory_space=pl.ANY)
    out = pl.pallas_call(
        functools.partial(
            _slab_kernel, places, gate_rows, groups, len(blocks), add_up, earlier is not None
        ),
        out_shape=out_shape,
        in_specs=[hbm] * (len(blocks) + 2 + len(extra)),
        out_specs=[hbm] * len(out_shape),
        scratch_shapes=[
            pltpu.VMEM((total, width), jnp.bfloat16),
            pltpu.VMEM((total, width), jnp.bfloat16),
            pltpu.VMEM((3 * units, width), jnp.bfloat16),
            pltpu.VMEM((total, 1), jnp.float32),
            *keep,
            pltpu.VMEM((total, width), jnp.bfloat16),
            pltpu.SemaphoreType.DMA((3 * n + 3,)),
            pltpu.SemaphoreType.DMA((2 + 2 * len(groups),)),
        ]
        + ([pltpu.VMEM((3 * units, width), jnp.bfloat16)] if add_up else []),
        compiler_params=pltpu.CompilerParams(vmem_limit_bytes=60 * MIB),
        cost_estimate=pl.CostEstimate(flops=1 << 20, bytes_accessed=1 << 16, transcendentals=0),
    )(*blocks, gate, w, *extra)
    return out[:n_first], out[n_first:]


def _weight_kernel(places, n_blocks, n_groups, more, *refs):
    blocks, refs = refs[:n_blocks], refs[n_blocks:]
    if more:
        earlier, refs = refs[0], refs[1:]
    grads, hiddens, refs = refs[:n_groups], refs[n_groups : 2 * n_groups], refs[2 * n_groups :]
    out, tok_v, cot_v, g_v, t_v, out_v, sem, sem_g, sem_out = refs
    n = len(places)
    total, width = tok_v.shape[0], tok_v.shape[1]
    rows = total // n
    units = out.shape[0] // 3
    small, at = [], 0
    for i in range(n_groups):
        size = hiddens[i].shape[0]
        here = pl.ds(at, size)
        small += [
            pltpu.make_async_copy(grads[i].at[0], g_v.at[0, here], sem_g.at[3 * i]),
            pltpu.make_async_copy(grads[i].at[1], g_v.at[1, here], sem_g.at[3 * i + 1]),
            pltpu.make_async_copy(hiddens[i], g_v.at[2, here], sem_g.at[3 * i + 2]),
        ]
        at += size
    large = [[], []]
    cut = width // 512 * 256
    for c, (start, size) in enumerate(((0, cut), (cut, width - cut))):
        cols = pl.ds(start, size)
        for p, (tb, tr, cb, cr) in enumerate(places):
            here = pl.ds(p * rows, rows)
            k = (c * n + p) * 2
            large[c] += [
                pltpu.make_async_copy(
                    blocks[tb].at[pl.ds(tr, rows), cols], tok_v.at[here, cols], sem.at[k]
                ),
                pltpu.make_async_copy(
                    blocks[cb].at[pl.ds(cr, rows), cols], cot_v.at[here, cols], sem.at[k + 1]
                ),
            ]
    if more:
        small.append(pltpu.make_async_copy(earlier, out_v, sem_g.at[3 * n_groups]))
    for copy in (*small, *large[0], *large[1]):
        copy.start()
    for copy in small:
        copy.wait()

    def turn(i, _):
        at = pl.multiple_of(i * 128, 128)
        for j in range(3):
            t_v[pl.ds(j * units, units), pl.ds(at, 128)] = g_v[j, pl.ds(at, 128)].T
        return 0

    lax.fori_loop(0, total // 128, turn, 0)
    outs = []
    for c, (start, size) in enumerate(((0, cut), (cut, width - cut))):
        for copy in large[c]:
            copy.wait()

        def tile(i, _, start=start):
            cols = pl.ds(pl.multiple_of(start + i * 256, 256), 256)
            left = jnp.dot(
                t_v[pl.ds(0, 2 * units)], tok_v[:, cols], preferred_element_type=jnp.float32
            )
            right = jnp.dot(
                t_v[pl.ds(2 * units, units)], cot_v[:, cols], preferred_element_type=jnp.float32
            )
            if more:
                left += out_v[pl.ds(0, 2 * units), cols].astype(jnp.float32)
                right += out_v[pl.ds(2 * units, units), cols].astype(jnp.float32)
            out_v[pl.ds(0, 2 * units), cols] = left.astype(jnp.bfloat16)
            out_v[pl.ds(2 * units, units), cols] = right.astype(jnp.bfloat16)
            return 0

        lax.fori_loop(0, size // 256, tile, 0)
        cols = pl.ds(start, size)
        outs.append(pltpu.make_async_copy(out_v.at[:, cols], out.at[:, cols], sem_out.at[c]))
        outs[-1].start()
    for copy in outs:
        copy.wait()


def weight_work(pieces, grads, hiddens, units, earlier=None):
    rows, width = 128, pieces[0][0].shape[1]
    blocks, places = [], []

    def place(array):
        for i, known in enumerate(blocks):
            if known is array:
                return i
        blocks.append(array)
        return len(blocks) - 1

    for tok, tr, cot, cr in pieces:
        places.append((place(tok), tr, place(cot), cr))
    n = len(pieces)
    total = n * rows
    extra = [] if earlier is None else [earlier]
    hbm = pl.BlockSpec(memory_space=pl.ANY)
    return pl.pallas_call(
        functools.partial(_weight_kernel, places, len(blocks), len(grads), earlier is not None),
        out_shape=jax.ShapeDtypeStruct((3 * units, width), jnp.bfloat16),
        in_specs=[hbm] * (len(blocks) + len(extra) + 2 * len(grads)),
        out_specs=hbm,
        scratch_shapes=[
            pltpu.VMEM((total, width), jnp.bfloat16),
            pltpu.VMEM((total, width), jnp.bfloat16),
            pltpu.VMEM((3, total, units), jnp.bfloat16),
            pltpu.VMEM((3 * units, total), jnp.bfloat16),
            pltpu.VMEM((3 * units, width), jnp.bfloat16),
            pltpu.SemaphoreType.DMA((4 * n,)),
            pltpu.SemaphoreType.DMA((3 * len(grads) + 1,)),
            pltpu.SemaphoreType.DMA((2,)),
        ],
        compiler_params=pltpu.CompilerParams(vmem_limit_bytes=60 * MIB),
        cost_estimate=pl.CostEstimate(flops=1 << 20, bytes_accessed=1 << 16, transcendentals=0),
    )(*blocks, *extra, *grads, *hiddens)


def gates_by_source(expert_ids, gates):
    n_x, n_z = lax.axis_size(X_AXIS), lax.axis_size(Z_AXIS)
    experts = jnp.arange(n_x, dtype=jnp.int32)
    dense = jnp.sum(
        jnp.where(expert_ids[None] == experts[:, None, None], gates[None], 0.0), axis=2
    )
    tokens_here = dense.shape[1]
    outgoing = jnp.broadcast_to(dense[:, None], (n_x, n_z, tokens_here))
    incoming = lax.all_to_all(
        outgoing.reshape(n_x * n_z, 1, tokens_here),
        (X_AXIS, Z_AXIS),
        split_axis=0,
        concat_axis=0,
        tiled=True,
    ).reshape(n_x, n_z, tokens_here)
    return incoming


def shards(tokens, grad_out, expert_ids, gates, weights):
    tokens, grad_out = tokens[0], grad_out[0]
    rows, width = tokens.shape
    half = width // 2
    mine_x, mine_z = lax.axis_index(X_AXIS), lax.axis_index(Z_AXIS)
    units = weights.shape[2]
    w = jnp.transpose(weights[0, 0], (1, 0, 2)).reshape(3 * units, width)
    own = jnp.concatenate([tokens, grad_out], axis=0)

    def hop_one(block):
        return send(block, X_AXIS, 1), send(block, X_AXIS, -1)

    def hop_two(prev, succ):
        return send(prev[:rows], X_AXIS, 1), send(succ[rows:], X_AXIS, -1)

    def add(*parts):
        return sum(p.astype(jnp.float32) for p in parts).astype(jnp.bfloat16)

    def out_one(first_half, second_half):
        return send(first_half, X_AXIS, 1), send(second_half, X_AXIS, -1)

    def out_two(near, from_prev, from_succ):
        prev, succ = near[rows : 2 * rows], near[2 * rows :]
        to_succ = jnp.concatenate([add(succ[:, :half], from_prev), succ[:, half:]], axis=1)
        to_prev = jnp.concatenate([prev[:, :half], add(prev[:, half:], from_succ)], axis=1)
        return send(to_succ, X_AXIS, 1), send(to_prev, X_AXIS, -1)

    n_pipe, n_z = lax.axis_size("pipe"), lax.axis_size(Z_AXIS)

    def home(total, z_distance):
        route = [
            (p * n_z + z, (p - 1) % n_pipe * n_z + (z - z_distance) % n_z)
            for p in range(n_pipe)
            for z in range(n_z)
        ]
        return lax.ppermute(total, ("pipe", Z_AXIS), route)

    def near(block, prev, succ):
        return [(b, 0, b, rows) for b in (block, prev, succ)]

    def far(tok, cot):
        return [(tok, 0, cot, 0)]

    def gate_rows(*numbers):
        return [i * rows for i in numbers]

    def tie(*values):
        return lax.optimization_barrier(values)

    scope = jax.named_scope
    with scope("z_prev"):
        z_prev = send(own, Z_AXIS, 1)
    with scope("first0"):
        first0 = hop_one(own)
    table = gates_by_source(after(expert_ids[0], own), gates[0]).reshape(-1, rows)
    order = [
        (mine_x - dx) % 4 * 4 + (mine_z - dz) % 4 for dz in (0, 1, -1, 2) for dx in (0, 1, -1, 2)
    ]
    gate = jnp.take(table, jnp.stack(order), axis=0).reshape(-1, 1)

    z_prev, gate, *first0 = tie(z_prev, gate, *first0)
    with scope("second0"):
        second0 = hop_two(*first0)
    with scope("first1"):
        first1 = hop_one(z_prev)
    with scope("z_next"):
        z_next = send(after(own, z_prev), Z_AXIS, -1)
    (part,), (near0,) = slab_work(
        near(own, *first0), gate, gate_rows(0, 1, 2), w, [(3, False)], True
    )

    z_next, near0, *second0 = tie(z_next, near0, *second0)
    with scope("first2"):
        first2 = hop_one(z_next)
    with scope("z_far"):
        z_far = (send(after(z_prev[:rows], z_next), Z_AXIS, 1), send(z_next[rows:], Z_AXIS, -1))

    near0, *first1 = tie(near0, *first1)
    with scope("second1"):
        second1 = hop_two(*first1)
    (part,), (far0, near1) = slab_work(
        far(*second0) + near(z_prev, *first1),
        after(gate, near0),
        gate_rows(3, 4, 5, 6),
        w,
        [(1, False), (3, False)],
        True,
        part,
    )

    far0, near1, *moved = tie(far0, near1, *first2, *second1, *z_far)
    first2, second1, z_far = moved[:2], moved[2:4], jnp.concatenate(moved[4:], axis=0)
    with scope("first3"):
        first3 = hop_one(z_far)
    with scope("home1_near"):
        home1_near = send(near1, Z_AXIS, -1)
    with scope("second2"):
        second2 = hop_two(*first2)
    (part,), (far1, near2) = slab_work(
        far(*second1) + near(z_next, *first2),
        gate,
        gate_rows(7, 8, 9, 10),
        w,
        [(1, False), (3, False)],
        True,
        part,
    )

    far1, near2, *moved = tie(far1, near2, *first3, *second2)
    first3, second2 = moved[:2], moved[2:]
    with scope("second3"):
        second3 = hop_two(*first3)
    with scope("home1_far"):
        home1_far = send(far1, Z_AXIS, -1)
    pieces3 = far(*second2) + near(z_far, *first3)
    (grads3, hidden3), (far2a, far2b, near3) = slab_work(
        pieces3, gate, gate_rows(11, 12, 13, 14), w, [(1, True), (3, False)]
    )
    with scope("one2"):
        one2 = out_one(far2a, far2b)
    near3, home1_far, *second3 = tie(near3, home1_far, *second3)
    far_own = add(far0, home1_far)
    near_own = add(near0, home1_near)
    with scope("one0"):
        one0 = out_one(far_own[:, :half], far_own[:, half:])
    pieces4 = far(*second3)
    (grads4, hidden4), (far3a, far3b) = slab_work(pieces4, gate, gate_rows(15), w, [(1, True)])
    with scope("one3"):
        one3 = out_one(far3a, far3b)
    with scope("two2"):
        two2 = out_two(near2, *one2)
    with scope("two0"):
        two0 = out_two(near_own, *one0)
    with scope("two3"):
        two3 = out_two(near3, *one3)
    with scope("total2"):
        total2 = home(add(near2[:rows], *two2), -1)
    with scope("total0"):
        total0 = home(add(near_own[:rows], *two0), 0)
    with scope("total3"):
        total3 = home(add(near3[:rows], *two3), 2)
    grad_prev = add(total0, total2, total3)[None]

    grad_weights = weight_work(
        pieces3 + pieces4, (grads3, grads4), (hidden3, after(hidden4, *two3)), units, part
    )
    grad_weights = jnp.transpose(grad_weights.reshape(3, units, width), (1, 0, 2))
    return grad_prev, grad_weights[None, None]


def solution(mesh):
    return jax.shard_map(
        shards,
        mesh=mesh,
        in_specs=(
            P("pipe", ("expert", "shard"), None),
            P("pipe", ("expert", "shard"), None),
            P("pipe", ("expert", "shard"), None),
            P("pipe", ("expert", "shard"), None),
            P("pipe", "expert", "shard", None, None),
        ),
        out_specs=(P("pipe", ("expert", "shard"), None), P("pipe", "expert", "shard", None, None)),
        check_vma=False,
    )
```

```python
import functools

import jax
import jax.numpy as jnp
from jax import lax
from jax.experimental import pallas as pl
from jax.experimental.pallas import tpu as pltpu
from jax.sharding import PartitionSpec as P

X_AXIS = "expert"
Z_AXIS = "shard"


def send(block, axis, distance):
    n = lax.axis_size(axis)
    return lax.ppermute(block, axis, [(i, (i + distance) % n) for i in range(n)])


def after(value, *earlier):
    return lax.optimization_barrier((value, *earlier))[0]


CONTRACT_LAST = (((1,), (1,)), ((), ()))
MIB = 1 << 20


def _slab_kernel(places, gate_rows, groups, n_blocks, add_up, more, *refs):
    blocks, (gate, w), refs = refs[:n_blocks], refs[n_blocks : n_blocks + 2], refs[n_blocks + 2 :]
    n = len(places)
    n_back = sum(2 if cut else 1 for _, cut in groups)
    if more:
        earlier, refs = refs[0], refs[1:]
    if add_up:
        grad_w, refs = refs[0], refs[1:]
    else:
        grads, hidden, refs = refs[0], refs[1], refs[2:]
    backs, refs = refs[:n_back], refs[n_back:]
    tok_v, cot_v, w_v, gate_v, g_v, h_v, back_v, sem_in, sem_out = refs[:9]
    rows = tok_v.shape[0] // n
    units = w.shape[0] // 3
    width = w.shape[1]

    toks, cots = [], []
    for p, (tb, tr, cb, cr) in enumerate(places):
        here = pl.ds(p * rows, rows)
        toks.append(pltpu.make_async_copy(blocks[tb].at[pl.ds(tr, rows)], tok_v.at[here], sem_in.at[p]))
        cots.append(
            pltpu.make_async_copy(blocks[cb].at[pl.ds(cr, rows)], cot_v.at[here], sem_in.at[n + p])
        )
    w_in = pltpu.make_async_copy(
        w.at[pl.ds(0, 2 * units)], w_v.at[pl.ds(0, 2 * units)], sem_in.at[3 * n]
    )
    w_down = pltpu.make_async_copy(
        w.at[pl.ds(2 * units, units)], w_v.at[pl.ds(2 * units, units)], sem_in.at[3 * n + 1]
    )
    gate_copy = pltpu.make_async_copy(gate, gate_v, sem_in.at[2 * n])
    for copy in (gate_copy, *toks, w_in, *cots, w_down):
        copy.start()
    if more:
        before = pltpu.make_async_copy(earlier, refs[9], sem_in.at[3 * n + 2])
        before.start()
    gate_copy.wait()
    columns = gate_v[...].T
    gate_here = jnp.concatenate([columns[:, i : i + 1] for i in gate_rows], axis=0)
    for copy in (*toks, w_in):
        copy.wait()
    w_gate, w_up = w_v[pl.ds(0, units)], w_v[pl.ds(units, units)]
    tok = tok_v[...]
    pre_gate = lax.dot_general(tok, w_gate, CONTRACT_LAST, preferred_element_type=jnp.float32)
    pre_up = lax.dot_general(tok, w_up, CONTRACT_LAST, preferred_element_type=jnp.float32)
    sig = jax.nn.sigmoid(pre_gate)
    gated = pre_gate * sig
    slope = sig * (1.0 + pre_gate * (1.0 - sig))
    for copy in (*cots, w_down):
        copy.wait()
    grad_hidden = gate_here * lax.dot_general(
        cot_v[...], w_v[pl.ds(2 * units, units)], CONTRACT_LAST, preferred_element_type=jnp.float32
    )
    hid = (gate_here * gated * pre_up).astype(jnp.bfloat16)
    grad_gate = (grad_hidden * pre_up * slope).astype(jnp.bfloat16)
    grad_up = (grad_hidden * gated).astype(jnp.bfloat16)
    outs = []
    if add_up:
        g_v[pl.ds(0, units)] = grad_gate.T
        g_v[pl.ds(units, units)] = grad_up.T
        h_v[...] = hid.T
    else:
        h_v[...] = hid
        g_v[0] = grad_gate
        g_v[1] = grad_up
        outs = [
            pltpu.make_async_copy(g_v, grads, sem_out.at[0]),
            pltpu.make_async_copy(h_v, hidden, sem_out.at[1]),
        ]
    for copy in outs:
        copy.start()
    half = width // 2
    for c in range(2):
        cols = pl.ds(c * half, half)
        back = jnp.dot(grad_gate, w_v[pl.ds(0, units), cols], preferred_element_type=jnp.float32)
        back += jnp.dot(grad_up, w_v[pl.ds(units, units), cols], preferred_element_type=jnp.float32)
        back_v[:, cols] = back.astype(jnp.bfloat16)
        at, row = 0, 0
        for k, (count, cut) in enumerate(groups):
            here = back_v.at[pl.ds(row, count * rows), cols]
            there = backs[at + c] if cut else backs[at].at[:, cols]
            outs.append(pltpu.make_async_copy(here, there, sem_out.at[2 + 2 * k + c]))
            outs[-1].start()
            at, row = at + (2 if cut else 1), row + count * rows
    if add_up:
        out_v = refs[9]
        if more:
            before.wait()

        def tile(i, _):
            cols = pl.ds(pl.multiple_of(i * 256, 256), 256)
            left = jnp.dot(g_v[...], tok_v[:, cols], preferred_element_type=jnp.float32)
            right = jnp.dot(h_v[...], cot_v[:, cols], preferred_element_type=jnp.float32)
            if more:
                left += out_v[pl.ds(0, 2 * units), cols].astype(jnp.float32)
                right += out_v[pl.ds(2 * units, units), cols].astype(jnp.float32)
            out_v[pl.ds(0, 2 * units), cols] = left.astype(jnp.bfloat16)
            out_v[pl.ds(2 * units, units), cols] = right.astype(jnp.bfloat16)
            return 0

        lax.fori_loop(0, width // 256, tile, 0)
        outs.append(pltpu.make_async_copy(out_v, grad_w, sem_out.at[0]))
        outs[-1].start()
    for copy in outs:
        copy.wait()


def slab_work(pieces, gate, gate_rows, w, groups, add_up=False, earlier=None):
    rows, width = 128, w.shape[1]
    units = w.shape[0] // 3
    blocks, places = [], []

    def place(array):
        for i, known in enumerate(blocks):
            if known is array:
                return i
        blocks.append(array)
        return len(blocks) - 1

    for tok, tr, cot, cr in pieces:
        places.append((place(tok), tr, place(cot), cr))
    n = len(pieces)
    total = n * rows
    if add_up:
        out_shape = [jax.ShapeDtypeStruct((3 * units, width), jnp.bfloat16)]
        keep = [pltpu.VMEM((2 * units, total), jnp.bfloat16), pltpu.VMEM((units, total), jnp.bfloat16)]
    else:
        out_shape = [
            jax.ShapeDtypeStruct((2, total, units), jnp.bfloat16),
            jax.ShapeDtypeStruct((total, units), jnp.bfloat16),
        ]
        keep = [pltpu.VMEM((2, total, units), jnp.bfloat16), pltpu.VMEM((total, units), jnp.bfloat16)]
    n_first = len(out_shape)
    for count, cut in groups:
        shape = (count * rows, width // 2) if cut else (count * rows, width)
        out_shape += [jax.ShapeDtypeStruct(shape, jnp.bfloat16)] * (2 if cut else 1)
    extra = [] if earlier is None else [earlier]
    hbm = pl.BlockSpec(memory_space=pl.ANY)
    out = pl.pallas_call(
        functools.partial(
            _slab_kernel, places, gate_rows, groups, len(blocks), add_up, earlier is not None
        ),
        out_shape=out_shape,
        in_specs=[hbm] * (len(blocks) + 2 + len(extra)),
        out_specs=[hbm] * len(out_shape),
        scratch_shapes=[
            pltpu.VMEM((total, width), jnp.bfloat16),
            pltpu.VMEM((total, width), jnp.bfloat16),
            pltpu.VMEM((3 * units, width), jnp.bfloat16),
            pltpu.VMEM(gate.shape, jnp.float32),
            *keep,
            pltpu.VMEM((total, width), jnp.bfloat16),
            pltpu.SemaphoreType.DMA((3 * n + 3,)),
            pltpu.SemaphoreType.DMA((2 + 2 * len(groups),)),
        ]
        + ([pltpu.VMEM((3 * units, width), jnp.bfloat16)] if add_up else []),
        compiler_params=pltpu.CompilerParams(vmem_limit_bytes=60 * MIB),
        cost_estimate=pl.CostEstimate(flops=1 << 20, bytes_accessed=1 << 16, transcendentals=0),
    )(*blocks, gate, w, *extra)
    return out[:n_first], out[n_first:]


def _weight_kernel(places, n_blocks, n_groups, more, *refs):
    blocks, refs = refs[:n_blocks], refs[n_blocks:]
    if more:
        earlier, refs = refs[0], refs[1:]
    grads, hiddens, refs = refs[:n_groups], refs[n_groups : 2 * n_groups], refs[2 * n_groups :]
    out, tok_v, cot_v, g_v, t_v, out_v, sem, sem_g, sem_out = refs
    n = len(places)
    total, width = tok_v.shape[0], tok_v.shape[1]
    rows = total // n
    units = out.shape[0] // 3
    small, at = [], 0
    for i in range(n_groups):
        size = hiddens[i].shape[0]
        here = pl.ds(at, size)
        small += [
            pltpu.make_async_copy(grads[i].at[0], g_v.at[0, here], sem_g.at[3 * i]),
            pltpu.make_async_copy(grads[i].at[1], g_v.at[1, here], sem_g.at[3 * i + 1]),
            pltpu.make_async_copy(hiddens[i], g_v.at[2, here], sem_g.at[3 * i + 2]),
        ]
        at += size
    large = [[], []]
    cut = width // 512 * 256
    for c, (start, size) in enumerate(((0, cut), (cut, width - cut))):
        cols = pl.ds(start, size)
        for p, (tb, tr, cb, cr) in enumerate(places):
            here = pl.ds(p * rows, rows)
            k = (c * n + p) * 2
            large[c] += [
                pltpu.make_async_copy(
                    blocks[tb].at[pl.ds(tr, rows), cols], tok_v.at[here, cols], sem.at[k]
                ),
                pltpu.make_async_copy(
                    blocks[cb].at[pl.ds(cr, rows), cols], cot_v.at[here, cols], sem.at[k + 1]
                ),
            ]
    if more:
        small.append(pltpu.make_async_copy(earlier, out_v, sem_g.at[3 * n_groups]))
    for copy in (*small, *large[0], *large[1]):
        copy.start()
    for copy in small:
        copy.wait()

    def turn(i, _):
        at = pl.multiple_of(i * 128, 128)
        for j in range(3):
            t_v[pl.ds(j * units, units), pl.ds(at, 128)] = g_v[j, pl.ds(at, 128)].T
        return 0

    lax.fori_loop(0, total // 128, turn, 0)
    outs = []
    for c, (start, size) in enumerate(((0, cut), (cut, width - cut))):
        for copy in large[c]:
            copy.wait()

        def tile(i, _, start=start):
            cols = pl.ds(pl.multiple_of(start + i * 256, 256), 256)
            left = jnp.dot(
                t_v[pl.ds(0, 2 * units)], tok_v[:, cols], preferred_element_type=jnp.float32
            )
            right = jnp.dot(
                t_v[pl.ds(2 * units, units)], cot_v[:, cols], preferred_element_type=jnp.float32
            )
            if more:
                left += out_v[pl.ds(0, 2 * units), cols].astype(jnp.float32)
                right += out_v[pl.ds(2 * units, units), cols].astype(jnp.float32)
            out_v[pl.ds(0, 2 * units), cols] = left.astype(jnp.bfloat16)
            out_v[pl.ds(2 * units, units), cols] = right.astype(jnp.bfloat16)
            return 0

        lax.fori_loop(0, size // 256, tile, 0)
        cols = pl.ds(start, size)
        outs.append(pltpu.make_async_copy(out_v.at[:, cols], out.at[:, cols], sem_out.at[c]))
        outs[-1].start()
    for copy in outs:
        copy.wait()


def weight_work(pieces, grads, hiddens, units, earlier=None):
    rows, width = 128, pieces[0][0].shape[1]
    blocks, places = [], []

    def place(array):
        for i, known in enumerate(blocks):
            if known is array:
                return i
        blocks.append(array)
        return len(blocks) - 1

    for tok, tr, cot, cr in pieces:
        places.append((place(tok), tr, place(cot), cr))
    n = len(pieces)
    total = n * rows
    extra = [] if earlier is None else [earlier]
    hbm = pl.BlockSpec(memory_space=pl.ANY)
    return pl.pallas_call(
        functools.partial(_weight_kernel, places, len(blocks), len(grads), earlier is not None),
        out_shape=jax.ShapeDtypeStruct((3 * units, width), jnp.bfloat16),
        in_specs=[hbm] * (len(blocks) + len(extra) + 2 * len(grads)),
        out_specs=hbm,
        scratch_shapes=[
            pltpu.VMEM((total, width), jnp.bfloat16),
            pltpu.VMEM((total, width), jnp.bfloat16),
            pltpu.VMEM((3, total, units), jnp.bfloat16),
            pltpu.VMEM((3 * units, total), jnp.bfloat16),
            pltpu.VMEM((3 * units, width), jnp.bfloat16),
            pltpu.SemaphoreType.DMA((4 * n,)),
            pltpu.SemaphoreType.DMA((3 * len(grads) + 1,)),
            pltpu.SemaphoreType.DMA((2,)),
        ],
        compiler_params=pltpu.CompilerParams(vmem_limit_bytes=60 * MIB),
        cost_estimate=pl.CostEstimate(flops=1 << 20, bytes_accessed=1 << 16, transcendentals=0),
    )(*blocks, *extra, *grads, *hiddens)


def gates_by_source(expert_ids, gates):
    n_x, n_z = lax.axis_size(X_AXIS), lax.axis_size(Z_AXIS)
    experts = jnp.arange(n_x, dtype=jnp.int32)
    dense = jnp.sum(
        jnp.where(expert_ids[None] == experts[:, None, None], gates[None], 0.0), axis=2
    )
    tokens_here = dense.shape[1]
    outgoing = jnp.broadcast_to(dense[:, None], (n_x, n_z, tokens_here))
    incoming = lax.all_to_all(
        outgoing.reshape(n_x * n_z, 1, tokens_here),
        (X_AXIS, Z_AXIS),
        split_axis=0,
        concat_axis=0,
        tiled=True,
    ).reshape(n_x, n_z, tokens_here)
    return incoming


def shards(tokens, grad_out, expert_ids, gates, weights):
    tokens, grad_out = tokens[0], grad_out[0]
    rows, width = tokens.shape
    half = width // 2
    mine_x, mine_z = lax.axis_index(X_AXIS), lax.axis_index(Z_AXIS)
    units = weights.shape[2]
    w = jnp.transpose(weights[0, 0], (1, 0, 2)).reshape(3 * units, width)
    own = jnp.concatenate([tokens, grad_out], axis=0)

    def hop_one(block):
        return send(block, X_AXIS, 1), send(block, X_AXIS, -1)

    def hop_two(prev, succ):
        return send(prev[:rows], X_AXIS, 1), send(succ[rows:], X_AXIS, -1)

    def add(*parts):
        return sum(p.astype(jnp.float32) for p in parts).astype(jnp.bfloat16)

    def out_one(first_half, second_half):
        return send(first_half, X_AXIS, 1), send(second_half, X_AXIS, -1)

    def out_two(near, from_prev, from_succ):
        prev, succ = near[rows : 2 * rows], near[2 * rows :]
        to_succ = jnp.concatenate([add(succ[:, :half], from_prev), succ[:, half:]], axis=1)
        to_prev = jnp.concatenate([prev[:, :half], add(prev[:, half:], from_succ)], axis=1)
        return send(to_succ, X_AXIS, 1), send(to_prev, X_AXIS, -1)

    n_pipe, n_z = lax.axis_size("pipe"), lax.axis_size(Z_AXIS)

    def home(total, z_distance):
        route = [
            (p * n_z + z, (p - 1) % n_pipe * n_z + (z - z_distance) % n_z)
            for p in range(n_pipe)
            for z in range(n_z)
        ]
        return lax.ppermute(total, ("pipe", Z_AXIS), route)

    def near(block, prev, succ):
        return [(b, 0, b, rows) for b in (block, prev, succ)]

    def far(tok, cot):
        return [(tok, 0, cot, 0)]

    def gate_rows(*numbers):
        return list(numbers)

    def tie(*values):
        return lax.optimization_barrier(values)

    scope = jax.named_scope
    with scope("z_prev"):
        z_prev = send(own, Z_AXIS, 1)
    with scope("first0"):
        first0 = hop_one(own)
    table = gates_by_source(after(expert_ids[0], own), gates[0]).reshape(-1, rows)
    order = [
        (mine_x - dx) % 4 * 4 + (mine_z - dz) % 4 for dz in (0, 1, -1, 2) for dx in (0, 1, -1, 2)
    ]
    gate = jnp.take(table, jnp.stack(order), axis=0)

    z_prev, gate, *first0 = tie(z_prev, gate, *first0)
    with scope("second0"):
        second0 = hop_two(*first0)
    with scope("first1"):
        first1 = hop_one(z_prev)
    with scope("z_next"):
        z_next = send(after(own, z_prev), Z_AXIS, -1)
    (part,), (near0,) = slab_work(
        near(own, *first0), gate, gate_rows(0, 1, 2), w, [(3, False)], True
    )

    z_next, near0, *second0 = tie(z_next, near0, *second0)
    with scope("first2"):
        first2 = hop_one(z_next)
    with scope("z_far"):
        z_far = (send(after(z_prev[:rows], z_next), Z_AXIS, 1), send(z_next[rows:], Z_AXIS, -1))

    near0, *first1 = tie(near0, *first1)
    with scope("second1"):
        second1 = hop_two(*first1)
    (part,), (far0, near1) = slab_work(
        far(*second0) + near(z_prev, *first1),
        after(gate, near0),
        gate_rows(3, 4, 5, 6),
        w,
        [(1, False), (3, False)],
        True,
        part,
    )

    with scope("home1_near"):
        home1_near = send(near1, Z_AXIS, -1)
    far0, near1, *moved = tie(far0, near1, *first2, *second1, *z_far)
    first2, second1, z_far = moved[:2], moved[2:4], jnp.concatenate(moved[4:], axis=0)
    with scope("first3"):
        first3 = hop_one(z_far)
    with scope("second2"):
        second2 = hop_two(*first2)
    (part,), (far1, near2) = slab_work(
        far(*second1) + near(z_next, *first2),
        gate,
        gate_rows(7, 8, 9, 10),
        w,
        [(1, False), (3, False)],
        True,
        part,
    )

    with scope("home1_far"):
        home1_far = send(far1, Z_AXIS, -1)
    far1, near2, home1_near, *moved = tie(far1, near2, home1_near, *first3, *second2)
    first3, second2 = moved[:2], moved[2:]
    tok3, cot3, gate = tie(first3[0][:rows], first3[1][rows:], gate)
    with scope("second3"):
        second3 = send(tok3, X_AXIS, 1), send(cot3, X_AXIS, -1)
    pieces3 = far(*second2) + near(z_far, *first3)
    (grads3, hidden3), (far2a, far2b, near3) = slab_work(
        pieces3, gate, gate_rows(11, 12, 13, 14), w, [(1, True), (3, False)]
    )
    with scope("one2"):
        one2 = out_one(far2a, far2b)
    near3, home1_far, *second3 = tie(near3, home1_far, *second3)
    far_own = add(far0, home1_far)
    with scope("one0"):
        one0 = out_one(far_own[:, :half], far_own[:, half:])
    pieces4 = far(*second3)
    (grads4, hidden4), (far3a, far3b) = slab_work(pieces4, gate, gate_rows(15), w, [(1, True)])
    far3a, far3b, home1_near, *one2 = tie(far3a, far3b, home1_near, *one2)
    near_own = add(near0, home1_near)
    with scope("one3"):
        one3 = out_one(far3a, far3b)
    with scope("two2"):
        two2 = out_two(near2, *one2)
    with scope("two0"):
        two0 = out_two(near_own, *one0)
    with scope("two3"):
        two3 = out_two(near3, *one3)
    with scope("total2"):
        total2 = send(add(near2[:rows], *two2), Z_AXIS, 1)
    with scope("total0"):
        total0 = home(add(near_own[:rows], *two0, total2), 0)
    with scope("total3"):
        total3 = home(add(near3[:rows], *two3), 2)
    grad_prev = add(total0, total3)[None]

    grad_weights = weight_work(
        pieces3 + pieces4, (grads3, grads4), (hidden3, after(hidden4, *two3)), units, part
    )
    grad_weights = jnp.transpose(grad_weights.reshape(3, units, width), (1, 0, 2))
    return grad_prev, grad_weights[None, None]


def solution(mesh):
    return jax.shard_map(
        shards,
        mesh=mesh,
        in_specs=(
            P("pipe", ("expert", "shard"), None),
            P("pipe", ("expert", "shard"), None),
            P("pipe", ("expert", "shard"), None),
            P("pipe", ("expert", "shard"), None),
            P("pipe", "expert", "shard", None, None),
        ),
        out_specs=(P("pipe", ("expert", "shard"), None), P("pipe", "expert", "shard", None, None)),
        check_vma=False,
    )
```

```python
import functools

import jax
import jax.numpy as jnp
from jax import lax
from jax.experimental import pallas as pl
from jax.experimental.pallas import tpu as pltpu
from jax.sharding import PartitionSpec as P

X_AXIS = "expert"
Z_AXIS = "shard"


def send(block, axis, distance):
    n = lax.axis_size(axis)
    return lax.ppermute(block, axis, [(i, (i + distance) % n) for i in range(n)])


def after(value, *earlier):
    return lax.optimization_barrier((value, *earlier))[0]


CONTRACT_LAST = (((1,), (1,)), ((), ()))
MIB = 1 << 20


def _slab_kernel(places, gate_rows, groups, n_blocks, add_up, more, *refs):
    blocks, (gate, w), refs = refs[:n_blocks], refs[n_blocks : n_blocks + 2], refs[n_blocks + 2 :]
    n = len(places)
    n_back = sum(2 if cut else 1 for _, cut in groups)
    if more:
        earlier, refs = refs[0], refs[1:]
    if add_up:
        grad_w, refs = refs[0], refs[1:]
    else:
        grads, hidden, refs = refs[0], refs[1], refs[2:]
    backs, refs = refs[:n_back], refs[n_back:]
    tok_v, cot_v, w_v, gate_v, g_v, h_v, back_v, sem_in, sem_out = refs[:9]
    rows = tok_v.shape[0] // n
    units = w.shape[0] // 3
    width = w.shape[1]

    toks, cots = [], []
    for p, (tb, tr, cb, cr) in enumerate(places):
        here = pl.ds(p * rows, rows)
        toks.append(pltpu.make_async_copy(blocks[tb].at[pl.ds(tr, rows)], tok_v.at[here], sem_in.at[p]))
        cots.append(
            pltpu.make_async_copy(blocks[cb].at[pl.ds(cr, rows)], cot_v.at[here], sem_in.at[n + p])
        )
    w_in = pltpu.make_async_copy(
        w.at[pl.ds(0, 2 * units)], w_v.at[pl.ds(0, 2 * units)], sem_in.at[3 * n]
    )
    w_down = pltpu.make_async_copy(
        w.at[pl.ds(2 * units, units)], w_v.at[pl.ds(2 * units, units)], sem_in.at[3 * n + 1]
    )
    gate_copy = pltpu.make_async_copy(gate, gate_v, sem_in.at[2 * n])
    for copy in (gate_copy, *toks, w_in, *cots, w_down):
        copy.start()
    if more:
        before = pltpu.make_async_copy(earlier, refs[9], sem_in.at[3 * n + 2])
        before.start()
    gate_copy.wait()
    columns = gate_v[...].T
    gate_here = jnp.concatenate([columns[:, i : i + 1] for i in gate_rows], axis=0)
    for copy in (*toks, w_in):
        copy.wait()
    w_gate, w_up = w_v[pl.ds(0, units)], w_v[pl.ds(units, units)]
    tok = tok_v[...]
    pre_gate = lax.dot_general(tok, w_gate, CONTRACT_LAST, preferred_element_type=jnp.float32)
    pre_up = lax.dot_general(tok, w_up, CONTRACT_LAST, preferred_element_type=jnp.float32)
    sig = jax.nn.sigmoid(pre_gate)
    gated = pre_gate * sig
    slope = sig * (1.0 + pre_gate * (1.0 - sig))
    for copy in (*cots, w_down):
        copy.wait()
    grad_hidden = gate_here * lax.dot_general(
        cot_v[...], w_v[pl.ds(2 * units, units)], CONTRACT_LAST, preferred_element_type=jnp.float32
    )
    hid = (gate_here * gated * pre_up).astype(jnp.bfloat16)
    grad_gate = (grad_hidden * pre_up * slope).astype(jnp.bfloat16)
    grad_up = (grad_hidden * gated).astype(jnp.bfloat16)
    outs = []
    if add_up:
        g_v[pl.ds(0, units)] = grad_gate.T
        g_v[pl.ds(units, units)] = grad_up.T
        h_v[...] = hid.T
    else:
        h_v[...] = hid
        g_v[0] = grad_gate
        g_v[1] = grad_up
        outs = [
            pltpu.make_async_copy(g_v, grads, sem_out.at[0]),
            pltpu.make_async_copy(h_v, hidden, sem_out.at[1]),
        ]
    for copy in outs:
        copy.start()
    half = width // 2
    for c in range(2):
        cols = pl.ds(c * half, half)
        back = jnp.dot(grad_gate, w_v[pl.ds(0, units), cols], preferred_element_type=jnp.float32)
        back += jnp.dot(grad_up, w_v[pl.ds(units, units), cols], preferred_element_type=jnp.float32)
        back_v[:, cols] = back.astype(jnp.bfloat16)
        at, row = 0, 0
        for k, (count, cut) in enumerate(groups):
            here = back_v.at[pl.ds(row, count * rows), cols]
            there = backs[at + c] if cut else backs[at].at[:, cols]
            outs.append(pltpu.make_async_copy(here, there, sem_out.at[2 + 2 * k + c]))
            outs[-1].start()
            at, row = at + (2 if cut else 1), row + count * rows
    if add_up:
        out_v = refs[9]
        if more:
            before.wait()

        def tile(i, _):
            cols = pl.ds(pl.multiple_of(i * 256, 256), 256)
            left = jnp.dot(g_v[...], tok_v[:, cols], preferred_element_type=jnp.float32)
            right = jnp.dot(h_v[...], cot_v[:, cols], preferred_element_type=jnp.float32)
            if more:
                left += out_v[pl.ds(0, 2 * units), cols].astype(jnp.float32)
                right += out_v[pl.ds(2 * units, units), cols].astype(jnp.float32)
            out_v[pl.ds(0, 2 * units), cols] = left.astype(jnp.bfloat16)
            out_v[pl.ds(2 * units, units), cols] = right.astype(jnp.bfloat16)
            return 0

        lax.fori_loop(0, width // 256, tile, 0)
        outs.append(pltpu.make_async_copy(out_v, grad_w, sem_out.at[0]))
        outs[-1].start()
    for copy in outs:
        copy.wait()


def slab_work(pieces, gate, gate_rows, w, groups, add_up=False, earlier=None):
    rows, width = 128, w.shape[1]
    units = w.shape[0] // 3
    blocks, places = [], []

    def place(array):
        for i, known in enumerate(blocks):
            if known is array:
                return i
        blocks.append(array)
        return len(blocks) - 1

    for tok, tr, cot, cr in pieces:
        places.append((place(tok), tr, place(cot), cr))
    n = len(pieces)
    total = n * rows
    if add_up:
        out_shape = [jax.ShapeDtypeStruct((3 * units, width), jnp.bfloat16)]
        keep = [pltpu.VMEM((2 * units, total), jnp.bfloat16), pltpu.VMEM((units, total), jnp.bfloat16)]
    else:
        out_shape = [
            jax.ShapeDtypeStruct((2, total, units), jnp.bfloat16),
            jax.ShapeDtypeStruct((total, units), jnp.bfloat16),
        ]
        keep = [pltpu.VMEM((2, total, units), jnp.bfloat16), pltpu.VMEM((total, units), jnp.bfloat16)]
    n_first = len(out_shape)
    for count, cut in groups:
        shape = (count * rows, width // 2) if cut else (count * rows, width)
        out_shape += [jax.ShapeDtypeStruct(shape, jnp.bfloat16)] * (2 if cut else 1)
    extra = [] if earlier is None else [earlier]
    hbm = pl.BlockSpec(memory_space=pl.ANY)
    out = pl.pallas_call(
        functools.partial(
            _slab_kernel, places, gate_rows, groups, len(blocks), add_up, earlier is not None
        ),
        out_shape=out_shape,
        in_specs=[hbm] * (len(blocks) + 2 + len(extra)),
        out_specs=[hbm] * len(out_shape),
        scratch_shapes=[
            pltpu.VMEM((total, width), jnp.bfloat16),
            pltpu.VMEM((total, width), jnp.bfloat16),
            pltpu.VMEM((3 * units, width), jnp.bfloat16),
            pltpu.VMEM(gate.shape, jnp.float32),
            *keep,
            pltpu.VMEM((total, width), jnp.bfloat16),
            pltpu.SemaphoreType.DMA((3 * n + 3,)),
            pltpu.SemaphoreType.DMA((2 + 2 * len(groups),)),
        ]
        + ([pltpu.VMEM((3 * units, width), jnp.bfloat16)] if add_up else []),
        compiler_params=pltpu.CompilerParams(vmem_limit_bytes=36 * MIB),
        cost_estimate=pl.CostEstimate(flops=1 << 20, bytes_accessed=1 << 16, transcendentals=0),
    )(*blocks, gate, w, *extra)
    return out[:n_first], out[n_first:]


def _weight_kernel(places, n_blocks, n_groups, more, *refs):
    blocks, refs = refs[:n_blocks], refs[n_blocks:]
    if more:
        earlier, refs = refs[0], refs[1:]
    grads, hiddens, refs = refs[:n_groups], refs[n_groups : 2 * n_groups], refs[2 * n_groups :]
    out, tok_v, cot_v, g_v, t_v, out_v, sem, sem_g, sem_out = refs
    n = len(places)
    total, width = tok_v.shape[0], tok_v.shape[1]
    rows = total // n
    units = out.shape[0] // 3
    small, at = [], 0
    for i in range(n_groups):
        size = hiddens[i].shape[0]
        here = pl.ds(at, size)
        small += [
            pltpu.make_async_copy(grads[i].at[0], g_v.at[0, here], sem_g.at[3 * i]),
            pltpu.make_async_copy(grads[i].at[1], g_v.at[1, here], sem_g.at[3 * i + 1]),
            pltpu.make_async_copy(hiddens[i], g_v.at[2, here], sem_g.at[3 * i + 2]),
        ]
        at += size
    large = [[], []]
    cut = width // 512 * 256
    for c, (start, size) in enumerate(((0, cut), (cut, width - cut))):
        cols = pl.ds(start, size)
        for p, (tb, tr, cb, cr) in enumerate(places):
            here = pl.ds(p * rows, rows)
            k = (c * n + p) * 2
            large[c] += [
                pltpu.make_async_copy(
                    blocks[tb].at[pl.ds(tr, rows), cols], tok_v.at[here, cols], sem.at[k]
                ),
                pltpu.make_async_copy(
                    blocks[cb].at[pl.ds(cr, rows), cols], cot_v.at[here, cols], sem.at[k + 1]
                ),
            ]
    if more:
        small.append(pltpu.make_async_copy(earlier, out_v, sem_g.at[3 * n_groups]))
    for copy in (*small, *large[0], *large[1]):
        copy.start()
    for copy in small:
        copy.wait()

    def turn(i, _):
        at = pl.multiple_of(i * 128, 128)
        for j in range(3):
            t_v[pl.ds(j * units, units), pl.ds(at, 128)] = g_v[j, pl.ds(at, 128)].T
        return 0

    lax.fori_loop(0, total // 128, turn, 0)
    outs = []
    for c, (start, size) in enumerate(((0, cut), (cut, width - cut))):
        for copy in large[c]:
            copy.wait()

        def tile(i, _, start=start):
            cols = pl.ds(pl.multiple_of(start + i * 256, 256), 256)
            left = jnp.dot(
                t_v[pl.ds(0, 2 * units)], tok_v[:, cols], preferred_element_type=jnp.float32
            )
            right = jnp.dot(
                t_v[pl.ds(2 * units, units)], cot_v[:, cols], preferred_element_type=jnp.float32
            )
            if more:
                left += out_v[pl.ds(0, 2 * units), cols].astype(jnp.float32)
                right += out_v[pl.ds(2 * units, units), cols].astype(jnp.float32)
            out_v[pl.ds(0, 2 * units), cols] = left.astype(jnp.bfloat16)
            out_v[pl.ds(2 * units, units), cols] = right.astype(jnp.bfloat16)
            return 0

        lax.fori_loop(0, size // 256, tile, 0)
        cols = pl.ds(start, size)
        outs.append(pltpu.make_async_copy(out_v.at[:, cols], out.at[:, cols], sem_out.at[c]))
        outs[-1].start()
    for copy in outs:
        copy.wait()


def weight_work(pieces, grads, hiddens, units, earlier=None):
    rows, width = 128, pieces[0][0].shape[1]
    blocks, places = [], []

    def place(array):
        for i, known in enumerate(blocks):
            if known is array:
                return i
        blocks.append(array)
        return len(blocks) - 1

    for tok, tr, cot, cr in pieces:
        places.append((place(tok), tr, place(cot), cr))
    n = len(pieces)
    total = n * rows
    extra = [] if earlier is None else [earlier]
    hbm = pl.BlockSpec(memory_space=pl.ANY)
    return pl.pallas_call(
        functools.partial(_weight_kernel, places, len(blocks), len(grads), earlier is not None),
        out_shape=jax.ShapeDtypeStruct((3 * units, width), jnp.bfloat16),
        in_specs=[hbm] * (len(blocks) + len(extra) + 2 * len(grads)),
        out_specs=hbm,
        scratch_shapes=[
            pltpu.VMEM((total, width), jnp.bfloat16),
            pltpu.VMEM((total, width), jnp.bfloat16),
            pltpu.VMEM((3, total, units), jnp.bfloat16),
            pltpu.VMEM((3 * units, total), jnp.bfloat16),
            pltpu.VMEM((3 * units, width), jnp.bfloat16),
            pltpu.SemaphoreType.DMA((4 * n,)),
            pltpu.SemaphoreType.DMA((3 * len(grads) + 1,)),
            pltpu.SemaphoreType.DMA((2,)),
        ],
        compiler_params=pltpu.CompilerParams(vmem_limit_bytes=36 * MIB),
        cost_estimate=pl.CostEstimate(flops=1 << 20, bytes_accessed=1 << 16, transcendentals=0),
    )(*blocks, *extra, *grads, *hiddens)


def gates_by_source(expert_ids, gates):
    n_x, n_z = lax.axis_size(X_AXIS), lax.axis_size(Z_AXIS)
    experts = jnp.arange(n_x, dtype=jnp.int32)
    dense = jnp.sum(
        jnp.where(expert_ids[None] == experts[:, None, None], gates[None], 0.0), axis=2
    )
    tokens_here = dense.shape[1]
    outgoing = jnp.broadcast_to(dense[:, None], (n_x, n_z, tokens_here))
    incoming = lax.all_to_all(
        outgoing.reshape(n_x * n_z, 1, tokens_here),
        (X_AXIS, Z_AXIS),
        split_axis=0,
        concat_axis=0,
        tiled=True,
    ).reshape(n_x, n_z, tokens_here)
    return incoming


def shards(tokens, grad_out, expert_ids, gates, weights):
    tokens, grad_out = tokens[0], grad_out[0]
    rows, width = tokens.shape
    half = width // 2
    mine_x, mine_z = lax.axis_index(X_AXIS), lax.axis_index(Z_AXIS)
    units = weights.shape[2]
    w = jnp.transpose(weights[0, 0], (1, 0, 2)).reshape(3 * units, width)
    own = jnp.concatenate([tokens, grad_out], axis=0)

    def hop_one(block):
        return send(block, X_AXIS, 1), send(block, X_AXIS, -1)

    def hop_two(prev, succ):
        return send(prev[:rows], X_AXIS, 1), send(succ[rows:], X_AXIS, -1)

    def add(*parts):
        return sum(p.astype(jnp.float32) for p in parts).astype(jnp.bfloat16)

    def out_one(first_half, second_half):
        return send(first_half, X_AXIS, 1), send(second_half, X_AXIS, -1)

    def out_two(near, from_prev, from_succ):
        prev, succ = near[rows : 2 * rows], near[2 * rows :]
        to_succ = jnp.concatenate([add(succ[:, :half], from_prev), succ[:, half:]], axis=1)
        to_prev = jnp.concatenate([prev[:, :half], add(prev[:, half:], from_succ)], axis=1)
        return send(to_succ, X_AXIS, 1), send(to_prev, X_AXIS, -1)

    n_pipe, n_z = lax.axis_size("pipe"), lax.axis_size(Z_AXIS)

    def home(total, z_distance):
        route = [
            (p * n_z + z, (p - 1) % n_pipe * n_z + (z - z_distance) % n_z)
            for p in range(n_pipe)
            for z in range(n_z)
        ]
        return lax.ppermute(total, ("pipe", Z_AXIS), route)

    def near(block, prev, succ):
        return [(b, 0, b, rows) for b in (block, prev, succ)]

    def far(tok, cot):
        return [(tok, 0, cot, 0)]

    def gate_rows(*numbers):
        return list(numbers)

    def tie(*values):
        return lax.optimization_barrier(values)

    scope = jax.named_scope
    with scope("z_prev"):
        z_prev = send(own, Z_AXIS, 1)
    with scope("first0"):
        first0 = hop_one(own)
    table = gates_by_source(after(expert_ids[0], own), gates[0]).reshape(-1, rows)
    order = [
        (mine_x - dx) % 4 * 4 + (mine_z - dz) % 4 for dz in (0, 1, -1, 2) for dx in (0, 1, -1, 2)
    ]
    gate = jnp.take(table, jnp.stack(order), axis=0)

    z_prev, gate, *first0 = tie(z_prev, gate, *first0)
    with scope("second0"):
        second0 = hop_two(*first0)
    with scope("first1"):
        first1 = hop_one(z_prev)
    with scope("z_next"):
        z_next = send(after(own, z_prev), Z_AXIS, -1)
    (part,), (near0,) = slab_work(
        near(own, *first0), gate, gate_rows(0, 1, 2), w, [(3, False)], True
    )

    z_next, near0 = tie(z_next, near0)
    with scope("first2"):
        first2 = hop_one(z_next)
    with scope("z_far"):
        z_far = (send(after(z_prev[:rows], z_next), Z_AXIS, 1), send(z_next[rows:], Z_AXIS, -1))

    near0, *first1 = tie(near0, *first1)
    with scope("second1"):
        second1 = hop_two(*first1)
    (part,), (far0, near1) = slab_work(
        far(*second0) + near(z_prev, *first1),
        after(gate, near0),
        gate_rows(3, 4, 5, 6),
        w,
        [(1, False), (3, False)],
        True,
        part,
    )

    with scope("home1_near"):
        home1_near = send(near1, Z_AXIS, -1)
    far0, near1, *moved = tie(far0, near1, *first2, *second1, *z_far)
    first2, second1, z_far = moved[:2], moved[2:4], jnp.concatenate(moved[4:], axis=0)
    with scope("first3"):
        first3 = hop_one(z_far)
    with scope("second2"):
        second2 = hop_two(*first2)
    (part,), (far1, near2) = slab_work(
        far(*second1) + near(z_next, *first2),
        gate,
        gate_rows(7, 8, 9, 10),
        w,
        [(1, False), (3, False)],
        True,
        part,
    )

    with scope("home1_far"):
        home1_far = send(far1, Z_AXIS, -1)
    far1, near2, home1_near, *moved = tie(far1, near2, home1_near, *first3, *second2)
    first3, second2 = moved[:2], moved[2:]
    tok3, cot3, gate = tie(first3[0][:rows], first3[1][rows:], gate)
    with scope("second3"):
        second3 = send(tok3, X_AXIS, 1), send(cot3, X_AXIS, -1)
    pieces3 = far(*second2) + near(z_far, *first3)
    (grads3, hidden3), (far2a, far2b, near3) = slab_work(
        pieces3, gate, gate_rows(11, 12, 13, 14), w, [(1, True), (3, False)]
    )
    with scope("one2"):
        one2 = out_one(far2a, far2b)
    near3, home1_far, *second3 = tie(near3, home1_far, *second3)
    far_own = add(far0, home1_far)
    with scope("one0"):
        one0 = out_one(far_own[:, :half], far_own[:, half:])
    pieces4 = far(*second3)
    (grads4, hidden4), (far3a, far3b) = slab_work(pieces4, gate, gate_rows(15), w, [(1, True)])
    far3a, far3b, home1_near, *one2 = tie(far3a, far3b, home1_near, *one2)
    near_own = add(near0, home1_near)
    with scope("one3"):
        one3 = out_one(far3a, far3b)
    with scope("two2"):
        two2 = out_two(near2, *one2)
    with scope("two0"):
        two0 = out_two(near_own, *one0)
    with scope("two3"):
        two3 = out_two(near3, *one3)
    with scope("total2"):
        total2 = send(add(near2[:rows], *two2), Z_AXIS, 1)
    with scope("total0"):
        total0 = home(add(near_own[:rows], *two0, total2), 0)
    with scope("total3"):
        total3 = home(add(near3[:rows], *two3), 2)
    grad_prev = add(total0, total3)[None]

    grad_weights = weight_work(
        pieces3 + pieces4, (grads3, grads4), (hidden3, after(hidden4, *two3)), units, part
    )
    grad_weights = jnp.transpose(grad_weights.reshape(3, units, width), (1, 0, 2))
    return grad_prev, grad_weights[None, None]


def solution(mesh):
    return jax.shard_map(
        shards,
        mesh=mesh,
        in_specs=(
            P("pipe", ("expert", "shard"), None),
            P("pipe", ("expert", "shard"), None),
            P("pipe", ("expert", "shard"), None),
            P("pipe", ("expert", "shard"), None),
            P("pipe", "expert", "shard", None, None),
        ),
        out_specs=(P("pipe", ("expert", "shard"), None), P("pipe", "expert", "shard", None, None)),
        check_vma=False,
    )
```
